32 devices in a mesh: grp: 2 (over y), rec: 4 (over z), chan: 2 (over x), fft: 2 (over core).
Axes of the slice: x: 2, y: 2, z: 4, core: 2. Of those that a mesh axis runs over, the one named last changes fastest.
Arguments:
- record_ids: int32 [8], P(('grp', 'rec')), parts along dimension 0, may hold values from 0 to 63
- rotations: float32 [64, 3, 3], replicated, as said below
- ligand_coords: int32 [3, 1024], P(None, 'grp'), parts along dimension 1, may hold values from -4096 to 4096
- atom_types: int32 [1024], P('grp'), parts along dimension 0, may hold values from 0 to 17
- channel_weights: float32 [18, 2], P(None, 'chan'), may hold values from -6 to 6
- receptor_spectra: float32 [4, 2, 2, 64, 4096], P('rec', 'chan', None, None, 'fft'), may hold values from -24 to 24
Outputs:
- energy: float32 [8, 64, 4096], P(('grp', 'rec'), 'fft', 'chan'), parts along dimension 0
The draws below stay inside these ranges and needn't reach their ends.
There are 2 independent parts, one for each index of `grp`. The reference program is written for one: setup_inputs(seed, part) draws one part's arguments, and reference() takes and returns one part's arrays. A program takes and returns all parts, laid end to end along the dimension named above; an argument that names none is the same for every part. Nothing has to cross between parts.
Inputs may be any that keep to these rules, and one draw needn't show every extreme that they name: `rotations`: each [3, 3] block is a rotation matrix: orthonormal with determinant 1.
All inputs are finite; a program needn't handle non-finite values.
Results may differ from the reference program's by a relative error of at most 0.0003.
Values sent between devices are 32-bit elements; how exact they have to be, the bound alone decides.
A program may use at most 64 MiB of HBM per device.

```python
import jax
import jax.numpy as jnp
from jax import lax

GRID = 64
ATOMS = 512
TYPES = 18
ROTS = 64
CH_DEV = 1
REC_DEV = 1
RECORDS_DEV = 1
CHANNELS = 2
RECEPTORS = 4
RECORDS = 4
N_REC = 4
N_CHAN = 2


def draw_rotations(key, part):
    quaternion = jax.random.normal(key, (ROTS, 4), dtype=jnp.float32) + 0.05
    quaternion = quaternion / jnp.sqrt(jnp.sum(quaternion * quaternion, axis=1, keepdims=True))
    quat_real = quaternion[:, 0]
    quat_first = quaternion[:, 1]
    quat_second = quaternion[:, 2]
    quat_third = quaternion[:, 3]
    entries = [1.0 - 2.0 * (quat_second * quat_second + quat_third * quat_third), 2.0 * (quat_first * quat_second - quat_real * quat_third), 2.0 * (quat_first * quat_third + quat_real * quat_second), 2.0 * (quat_first * quat_second + quat_real * quat_third), 1.0 - 2.0 * (quat_first * quat_first + quat_third * quat_third), 2.0 * (quat_second * quat_third - quat_real * quat_first), 2.0 * (quat_first * quat_third - quat_real * quat_second), 2.0 * (quat_second * quat_third + quat_real * quat_first), 1.0 - 2.0 * (quat_first * quat_first + quat_second * quat_second)]
    return jnp.stack(entries, axis=1).reshape(ROTS, 3, 3)


def touch_ends(array, rng, low, largest):
    index_at = [jax.random.randint(jax.random.fold_in(rng, axis), (), 0, length) for axis, length in enumerate(array.shape)]
    main_axis = array.shape.index(max(array.shape))
    next_to = index_at[:main_axis] + [(index_at[main_axis] + 1) % array.shape[main_axis]] + index_at[main_axis + 1:]
    return array.at[tuple(index_at)].set(low).at[tuple(next_to)].set(largest)


def block_scale(stream_key, extent, pieces, low, top_value):
    loudness, own = 1.0, jax.random.fold_in(stream_key, 6)
    for position, blocks in pieces:
        heights = jnp.exp(jax.random.uniform(jax.random.fold_in(own, position), (blocks,), jnp.float32, low / len(pieces), top_value / len(pieces)))
        loudness = loudness * jnp.repeat(heights, extent[position] // blocks).reshape([-1 if axis == position else 1 for axis in range(len(extent))])
    return loudness


def centred(stream_key, extent, scale, limit, pieces=(), kind=jnp.bfloat16):
    factor_of = block_scale(stream_key, extent, pieces, -0.22, 0.18) if pieces else 1.0
    result = jax.random.normal(stream_key, extent, jnp.float32) * scale * factor_of
    return jnp.minimum(jnp.maximum(result, -limit), limit).astype(kind)


def setup_inputs(seed: int = 0, part: int = 0) -> dict:
    key_of = jax.random.split(jax.random.key(seed), 7)
    part_splits = jax.random.split(jax.random.fold_in(key_of[6], part), 7)
    return {
        "record_ids": touch_ends(jax.random.randint(part_splits[0], (RECORDS,), 0, ROTS), jax.random.fold_in(part_splits[0], 1), 0, ROTS - 1).astype(jnp.int32),
        "rotations": draw_rotations(jax.random.fold_in(key_of[6], 71), part),
        "ligand_coords": touch_ends(jax.random.randint(part_splits[2], (3, ATOMS), -(GRID // 4) * 256, (GRID // 4) * 256 + 1), jax.random.fold_in(part_splits[2], 1), -(GRID // 4) * 256, ((GRID // 4) * 256 + 1) - 1).astype(jnp.int32),
        "atom_types": touch_ends(jax.random.randint(part_splits[3], (ATOMS,), 0, TYPES), jax.random.fold_in(part_splits[3], 1), 0, TYPES - 1).astype(jnp.int32),
        "channel_weights": centred(key_of[4], (TYPES, CHANNELS), 1.0, 6.0, ((1, 2),), jnp.float32),
        "receptor_spectra": centred(key_of[5], (RECEPTORS, CHANNELS, 2, GRID, GRID * GRID), 4.0, 24.0, ((0, 4), (1, 2), (4, 2)), jnp.float32),
    }


def hat_rows(places, count):
    cells = jnp.arange(count).astype(jnp.float32)
    return jnp.maximum(0.0, 1.0 - jnp.abs(places[:, None] - cells[None, :]))


def reference(record_ids, rotations, ligand_coords, atom_types, channel_weights, receptor_spectra):
    channels = CH_DEV * N_CHAN
    coords = ligand_coords.astype(jnp.float32) * (1.0 / 256.0)
    atom_weights = channel_weights[atom_types]
    grouped = receptor_spectra.reshape(N_REC, REC_DEV, channels, 2, GRID, GRID, GRID)
    device_sums = jnp.sum(grouped, axis=1)
    window = device_sums + jnp.roll(device_sums, -1, axis=0) + jnp.roll(device_sums, -2, axis=0)
    spectra = lax.complex(window[:, :, 0], window[:, :, 1])

    def score_record(index):
        matrix = rotations[record_ids[index]]
        places = [0.5 * GRID + (matrix[axis_row, 0] * coords[0] + matrix[axis_row, 1] * coords[1] + matrix[axis_row, 2] * coords[2]) for axis_row in range(3)]
        grid = jnp.einsum('ac,ax,ay,az->cxyz', atom_weights, hat_rows(places[0], GRID), hat_rows(places[1], GRID), hat_rows(places[2], GRID), precision=lax.Precision.HIGHEST)
        ligand = jnp.fft.fftn(grid, axes=(1, 2, 3))
        home = index // RECORDS_DEV
        product = jnp.sum(jnp.conj(ligand) * spectra[home], axis=0)
        return jnp.real(jnp.fft.ifftn(product)).reshape(GRID, GRID * GRID)

    scores = lax.map(score_record, jnp.arange(record_ids.shape[0], dtype=jnp.int32))
    return jnp.roll(scores, 2 * RECORDS_DEV, axis=0)
```

```python
import math

import jax
import jax.numpy as jnp
from jax import lax
from jax.sharding import PartitionSpec as P

GRID = 64
HALF = GRID // 2
HIGHEST = lax.Precision.HIGHEST
HIGH = lax.Precision.HIGH


def from_behind(value, axis, steps):
    count = lax.axis_size(axis)
    pairs = [(source, (source + steps) % count) for source in range(count)]
    return lax.ppermute(value, axis, pairs)


def waves(rows, columns):
    phase = rows[:, None] * columns[None, :] % GRID
    angle = phase.astype(jnp.float32) * (2.0 * math.pi / GRID)
    return jnp.cos(angle), jnp.sin(angle)


def hat_rows(places, cells):
    return jnp.maximum(0.0, 1.0 - jnp.abs(places[:, None] - cells[None, :]))


def fold(receptor, width):
    lane = jnp.arange(width, dtype=jnp.int32)
    upper = receptor[:, HALF:]
    other = lax.ppermute(upper, "fft", [(0, 1), (1, 0)])
    source = jnp.where(lane < GRID, upper, other)
    back = lax.rev(source, (1, 2))
    mirrored = jnp.where(lane % GRID == 0, jnp.roll(back, 1, axis=2), jnp.roll(back, 65, axis=2))
    sign = jnp.array([1.0, -1.0], jnp.float32)[:, None, None]
    inner = mirrored[:, : HALF - 1] * sign
    inner = jnp.pad(inner, ((0, 0), (1, 1), (0, 0)))
    return receptor[:, : HALF + 1] + inner


def ligand_spectrum(record, rotations, ligand_coords, atom_types, channel_weights, width):
    table_rows = rotations.shape[0]
    picks = (record[:, None] == jnp.arange(table_rows, dtype=jnp.int32)[None, :]).astype(
        jnp.float32
    )
    matrix = jnp.dot(picks, rotations.reshape(table_rows, 9), precision=HIGHEST)[0]
    kinds = channel_weights.shape[0]
    type_hot = (atom_types[:, None] == jnp.arange(kinds, dtype=jnp.int32)[None, :]).astype(
        jnp.float32
    )
    weights = jnp.dot(type_hot, channel_weights, precision=HIGHEST)
    coords = ligand_coords.astype(jnp.float32) * (1.0 / 256.0)
    cells = jnp.arange(GRID, dtype=jnp.float32)
    hats = []
    for row in range(3):
        places = 0.5 * GRID + (
            matrix[3 * row] * coords[0]
            + matrix[3 * row + 1] * coords[1]
            + matrix[3 * row + 2] * coords[2]
        )
        hats.append(hat_rows(places, cells))
    index = jnp.arange(GRID, dtype=jnp.int32)
    lane = jnp.arange(width, dtype=jnp.int32)
    ky = lane // GRID + lax.axis_index("fft") * (width // GRID)
    y_cos, y_sin = waves(index, ky)
    z_cos, z_sin = waves(index, lane % GRID)
    x_cos, x_sin = waves(index, jnp.arange(HALF + 1, dtype=jnp.int32))
    y_hat = hats[1] * weights
    y_re = jnp.dot(y_hat, y_cos, precision=HIGH)
    y_im = jnp.dot(y_hat, y_sin, precision=HIGH)
    z_re = jnp.dot(hats[2], z_cos, precision=HIGH)
    z_im = jnp.dot(hats[2], z_sin, precision=HIGH)
    v_re = y_re * z_re - y_im * z_im
    v_im = y_re * z_im + y_im * z_re
    x_re = jnp.einsum("ax,xk->ka", hats[0], x_cos, precision=HIGH)
    x_im = jnp.einsum("ax,xk->ka", hats[0], x_sin, precision=HIGH)
    real = jnp.dot(x_re, v_re, precision=HIGH) - jnp.dot(x_im, v_im, precision=HIGH)
    imaginary = jnp.dot(x_re, v_im, precision=HIGH) + jnp.dot(x_im, v_re, precision=HIGH)
    return real, imaginary


def body(record_ids, rotations, ligand_coords, atom_types, channel_weights, receptor_spectra):
    width = receptor_spectra.shape[-1]
    slab = GRID // lax.axis_size("fft")
    record = from_behind(record_ids, "rec", 2)
    folded = fold(receptor_spectra[0, 0], width)
    pair = folded + from_behind(folded, "rec", 1)
    window = folded + from_behind(pair, "rec", 1)
    lig_re, lig_im = ligand_spectrum(
        record, rotations, ligand_coords, atom_types, channel_weights, width
    )
    product_re = lig_re * window[0] - lig_im * window[1]
    product_im = lig_re * window[1] + lig_im * window[0]
    index = jnp.arange(GRID, dtype=jnp.int32)
    cosine, sine = waves(index, jnp.arange(HALF + 1, dtype=jnp.int32))
    product = jnp.concatenate([product_re, product_im], axis=0)
    scale = 1.0 / float(GRID**3)
    turn = (
        jnp.concatenate(
            [
                jnp.concatenate([cosine, -sine], axis=1),
                jnp.concatenate([sine, cosine], axis=1),
            ],
            axis=0,
        )
        * scale
    )
    turned = jnp.dot(turn, product, precision=HIGH).reshape(1, 2, GRID, width)
    halves = lax.all_to_all(turned, "fft", split_axis=2, concat_axis=3, tiled=True)
    volume = halves.reshape(2, slab, GRID, GRID)
    cosine, sine = waves(index, index)
    y_turn = jnp.stack([jnp.stack([cosine, -sine]), jnp.stack([sine, cosine])])
    in_y = jnp.einsum("dcky,cxkz->dxyz", y_turn, volume, precision=HIGH)
    z_turn = jnp.stack([cosine, -sine])
    scores = jnp.einsum("dxyz,dzt->xyt", in_y, z_turn, precision=HIGH)
    summed = scores.reshape(1, slab, GRID * GRID)
    return lax.psum_scatter(summed, "chan", scatter_dimension=2, tiled=True)


def solution(mesh):
    in_specs = (
        P(("grp", "rec")),
        P(),
        P(None, "grp"),
        P("grp"),
        P(None, "chan"),
        P("rec", "chan", None, None, "fft"),
    )
    out_specs = P(("grp", "rec"), "fft", "chan")
    return jax.shard_map(body, mesh=mesh, in_specs=in_specs, out_specs=out_specs, check_vma=False)
```

```python
import math

import jax
import jax.numpy as jnp
from jax import lax
from jax.sharding import PartitionSpec as P

GRID = 64
HALF = GRID // 2
HIGHEST = lax.Precision.HIGHEST
HIGH = lax.Precision.HIGH


def from_behind(value, axis, steps):
    count = lax.axis_size(axis)
    pairs = [(source, (source + steps) % count) for source in range(count)]
    return lax.ppermute(value, axis, pairs)


def waves(rows, columns):
    phase = rows[:, None] * columns[None, :] % GRID
    angle = phase.astype(jnp.float32) * (2.0 * math.pi / GRID)
    return jnp.cos(angle), jnp.sin(angle)


def hat_rows(places, cells):
    return jnp.maximum(0.0, 1.0 - jnp.abs(places[:, None] - cells[None, :]))


def fold(receptor, width):
    lane = jnp.arange(width, dtype=jnp.int32)
    upper = receptor[:, HALF:]
    other = lax.ppermute(upper, "fft", [(0, 1), (1, 0)])
    source = jnp.where(lane < GRID, upper, other)
    back = lax.rev(source, (1, 2))
    mirrored = jnp.where(lane % GRID == 0, jnp.roll(back, 1, axis=2), jnp.roll(back, 65, axis=2))
    sign = jnp.array([1.0, -1.0], jnp.float32)[:, None, None]
    inner = mirrored[:, : HALF - 1] * sign
    inner = jnp.pad(inner, ((0, 0), (1, 1), (0, 0)))
    return receptor[:, : HALF + 1] + inner


def ligand_spectrum(record, rotations, ligand_coords, atom_types, channel_weights, width):
    table_rows = rotations.shape[0]
    picks = (record[:, None] == jnp.arange(table_rows, dtype=jnp.int32)[None, :]).astype(
        jnp.float32
    )
    matrix = jnp.dot(picks, rotations.reshape(table_rows, 9), precision=HIGHEST)[0]
    kinds = channel_weights.shape[0]
    type_hot = (atom_types[:, None] == jnp.arange(kinds, dtype=jnp.int32)[None, :]).astype(
        jnp.float32
    )
    weights = jnp.dot(type_hot, channel_weights, precision=HIGHEST)
    coords = ligand_coords.astype(jnp.float32) * (1.0 / 256.0)
    cells = jnp.arange(GRID, dtype=jnp.float32)
    hats = []
    for row in range(3):
        places = 0.5 * GRID + (
            matrix[3 * row] * coords[0]
            + matrix[3 * row + 1] * coords[1]
            + matrix[3 * row + 2] * coords[2]
        )
        hats.append(hat_rows(places, cells))
    index = jnp.arange(GRID, dtype=jnp.int32)
    lane = jnp.arange(width, dtype=jnp.int32)
    ky = lane // GRID + lax.axis_index("fft") * (width // GRID)
    y_cos, y_sin = waves(index, ky)
    z_cos, z_sin = waves(index, lane % GRID)
    x_cos, x_sin = waves(index, jnp.arange(HALF + 1, dtype=jnp.int32))
    y_hat = hats[1] * weights
    y_re = jnp.dot(y_hat, y_cos, precision=HIGH)
    y_im = jnp.dot(y_hat, y_sin, precision=HIGH)
    z_re = jnp.dot(hats[2], z_cos, precision=HIGH)
    z_im = jnp.dot(hats[2], z_sin, precision=HIGH)
    v_re = y_re * z_re - y_im * z_im
    v_im = y_re * z_im + y_im * z_re
    x_re = jnp.einsum("ax,xk->ka", hats[0], x_cos, precision=HIGH)
    x_im = jnp.einsum("ax,xk->ka", hats[0], x_sin, precision=HIGH)
    real = jnp.dot(x_re, v_re, precision=HIGH) - jnp.dot(x_im, v_im, precision=HIGH)
    imaginary = jnp.dot(x_re, v_im, precision=HIGH) + jnp.dot(x_im, v_re, precision=HIGH)
    return real, imaginary


def body(record_ids, rotations, ligand_coords, atom_types, channel_weights, receptor_spectra):
    width = receptor_spectra.shape[-1]
    slab = GRID // lax.axis_size("fft")
    record = from_behind(record_ids, "rec", 2)
    folded = fold(receptor_spectra[0, 0], width)
    folded, record, coords, types, weights = lax.optimization_barrier(
        (folded, record, ligand_coords, atom_types, channel_weights)
    )
    pair = folded + from_behind(folded, "rec", 1)
    window = folded + from_behind(pair, "rec", 1)
    lig_re, lig_im = ligand_spectrum(record, rotations, coords, types, weights, width)
    product_re = lig_re * window[0] - lig_im * window[1]
    product_im = lig_re * window[1] + lig_im * window[0]
    index = jnp.arange(GRID, dtype=jnp.int32)
    cosine, sine = waves(index, jnp.arange(HALF + 1, dtype=jnp.int32))
    product = jnp.concatenate([product_re, product_im], axis=0)
    scale = 1.0 / float(GRID**3)
    turn = (
        jnp.concatenate(
            [
                jnp.concatenate([cosine, -sine], axis=1),
                jnp.concatenate([sine, cosine], axis=1),
            ],
            axis=0,
        )
        * scale
    )
    turned = jnp.dot(turn, product, precision=HIGH).reshape(1, 2, GRID, width)
    halves = lax.all_to_all(turned, "fft", split_axis=2, concat_axis=3, tiled=True)
    volume = halves.reshape(2, slab, GRID, GRID)
    cosine, sine = waves(index, index)
    z_turn = jnp.stack([cosine, -sine])

    def scores(places):
        y_cos, y_sin = waves(index, places)
        y_turn = jnp.stack([jnp.stack([y_cos, -y_sin]), jnp.stack([y_sin, y_cos])])
        in_y = jnp.einsum("dcky,cxkz->dxyz", y_turn, volume, precision=HIGH)
        part = jnp.einsum("dxyz,dzt->xyt", in_y, z_turn, precision=HIGH)
        return part.reshape(1, slab, places.shape[0] * GRID)

    count = lax.axis_size("chan")
    if count != 2:
        return lax.psum_scatter(scores(index), "chan", scatter_dimension=2, tiled=True)
    near = lax.axis_index("chan") * HALF + jnp.arange(HALF, dtype=jnp.int32)
    far = (near + HALF) % GRID
    arrived = from_behind(scores(far), "chan", 1)
    return scores(near) + arrived


def solution(mesh):
    in_specs = (
        P(("grp", "rec")),
        P(),
        P(None, "grp"),
        P("grp"),
        P(None, "chan"),
        P("rec", "chan", None, None, "fft"),
    )
    out_specs = P(("grp", "rec"), "fft", "chan")
    return jax.shard_map(body, mesh=mesh, in_specs=in_specs, out_specs=out_specs, check_vma=False)
```

```python
import math

import functools

import jax
import jax.numpy as jnp
import numpy as np
from jax import lax
from jax.experimental import pallas as pl
from jax.experimental.pallas import tpu as pltpu
from jax.sharding import PartitionSpec as P

GRID = 64
HALF = GRID // 2
HIGHEST = lax.Precision.HIGHEST
HIGH = lax.Precision.HIGH


def from_behind(value, axis, steps):
    count = lax.axis_size(axis)
    pairs = [(source, (source + steps) % count) for source in range(count)]
    return lax.ppermute(value, axis, pairs)


def waves(rows, columns):
    phase = rows[:, None] * columns[None, :] % GRID
    angle = phase.astype(jnp.float32) * (2.0 * math.pi / GRID)
    return jnp.cos(angle), jnp.sin(angle)


def hat_rows(places, cells):
    return jnp.maximum(0.0, 1.0 - jnp.abs(places[:, None] - cells[None, :]))


def fold(receptor, width):
    lane = jnp.arange(width, dtype=jnp.int32)
    upper = receptor[:, HALF:]
    other = lax.ppermute(upper, "fft", [(0, 1), (1, 0)])
    source = jnp.where(lane < GRID, upper, other)
    back = lax.rev(source, (1, 2))
    mirrored = jnp.where(lane % GRID == 0, jnp.roll(back, 1, axis=2), jnp.roll(back, 65, axis=2))
    sign = jnp.array([1.0, -1.0], jnp.float32)[:, None, None]
    inner = mirrored[:, : HALF - 1] * sign
    inner = jnp.pad(inner, ((0, 0), (1, 1), (0, 0)))
    return receptor[:, : HALF + 1] + inner


def host_waves(rows, columns):
    angle = (np.outer(rows, columns) % GRID) * (2.0 * np.pi / GRID)
    return np.cos(angle), np.sin(angle)


def tripled(table):
    table = table.astype(np.float32)
    high = table.astype(jnp.bfloat16)
    low = (table - high.astype(np.float32)).astype(jnp.bfloat16)
    return np.concatenate([high, high, low], axis=0)


ROWS = 72
LANES = 256


def split(value):
    high = value.astype(jnp.bfloat16)
    return high, (value - high.astype(jnp.float32)).astype(jnp.bfloat16)


def dot(left, right):
    return jnp.dot(left, right, preferred_element_type=jnp.float32)


def window_kernel(
    count, g_ref, l_ref, y_ref, z_ref, yt_ref, zt_ref, turn_ref, out_ref,
    own, first, pair, second, win, lig, z_wave, l_high, l_low,
    send1, recv1, send2, recv2, send3, recv3,
):
    grp = lax.axis_index("grp")
    rec = lax.axis_index("rec")
    after = lax.rem(rec + 1, count)
    before = lax.rem(rec + count - 1, count)
    chunks = own.shape[0]
    mine = chunks // 2
    barrier = pltpu.get_barrier_semaphore()
    for target in ({"rec": after}, {"rec": before}, {"grp": 1 - grp}):
        pl.semaphore_signal(
            barrier, inc=1, device_id=target, device_id_type=pl.DeviceIdType.MESH
        )
    for chunk in range(chunks):
        own[chunk] = g_ref[:, chunk * LANES : (chunk + 1) * LANES]
    pl.semaphore_wait(barrier, 3)
    base = grp * mine

    def remote(source, target, send, recv, device):
        return pltpu.make_async_remote_copy(
            src_ref=source, dst_ref=target, send_sem=send, recv_sem=recv,
            device_id=device, device_id_type=pl.DeviceIdType.MESH,
        )

    ones = [
        remote(own.at[base + c], first.at[c], send1.at[c], recv1.at[c], {"rec": after})
        for c in range(mine)
    ]
    twos = [
        remote(pair.at[c], second.at[c], send2.at[c], recv2.at[c], {"rec": after})
        for c in range(mine)
    ]
    threes = [
        remote(win.at[base + c], win.at[base + c], send3.at[c], recv3.at[c], {"grp": 1 - grp})
        for c in range(mine)
    ]
    for copy in ones:
        copy.start()

    z_wave[...] = dot(z_ref[...], zt_ref[...])
    high, low = split(l_ref[...])
    l_high[...] = high
    l_low[...] = low

    def ligand(chunk):
        y_wave = dot(y_ref[...], yt_ref[chunk])
        y_re, y_im = y_wave[:, :LANES], y_wave[:, LANES:]
        z_re, z_im = z_wave[:, :LANES], z_wave[:, LANES:]
        re_high, re_low = split(y_re * z_re - y_im * z_im)
        im_high, im_low = split(y_re * z_im + y_im * z_re)
        v_high = jnp.concatenate([re_high, im_high], axis=0)
        v_low = jnp.concatenate([re_low, im_low], axis=0)
        lig[chunk] = (
            dot(l_high[...], v_high) + dot(l_low[...], v_high) + dot(l_high[...], v_low)
        )

    t_high, t_low = split(turn_ref[...])

    def product(chunk):
        l_re, l_im = lig[chunk, 0:32], lig[chunk, 32:64]
        w_re, w_im = win[chunk, 0:32], win[chunk, 32:64]
        tail_l, tail_w = lig[chunk, 64:72], win[chunk, 64:72]
        a, b = tail_l[0:1], tail_l[1:2]
        c, d = tail_w[0:1], tail_w[1:2]
        row = lax.broadcasted_iota(jnp.int32, (8, LANES), 0)
        tail = jnp.where(row == 0, a * c - b * d, jnp.where(row == 1, a * d + b * c, 0.0))
        whole = jnp.concatenate([l_re * w_re - l_im * w_im, l_re * w_im + l_im * w_re, tail], axis=0)
        p_high, p_low = split(whole)
        lanes = pl.ds(pl.multiple_of(chunk * LANES, LANES), LANES)
        out_ref[:, lanes] = dot(t_high, p_high) + dot(t_low, p_high) + dot(t_high, p_low)

    ligand(0)
    ligand(1)
    ligand(2)
    for c in range(mine):
        ones[c].wait_recv()
        pair[c] = own[base + c] + first[c]
        twos[c].start()
        ligand(3 + c)
    ligand(7)
    for c in range(mine):
        twos[c].wait_recv()
        win[base + c] = own[base + c] + second[c]
        threes[c].start()
        product(base + c)
    for c in range(mine):
        threes[c].wait_recv()
        product((1 - grp) * mine + c)
    for copy in ones + twos + threes:
        copy.wait_send()


def turned_product(folded, left, y_hat, z_hat, width):
    index = np.arange(GRID)
    chunks = width // LANES
    lane = np.arange(width)
    cosine, sine = host_waves(index, lane // GRID)
    y_table = np.stack(
        [
            tripled(
                np.concatenate(
                    [t[:, c * LANES : (c + 1) * LANES] for t in (cosine, sine)], axis=1
                )
            )
            for c in range(chunks)
        ]
    )
    z_table = tripled(np.concatenate(host_waves(index, lane[:LANES] % GRID), axis=1))
    cosine, sine = host_waves(index, np.arange(HALF + 1))
    real = np.concatenate([cosine[:, :HALF], -sine[:, :HALF], cosine[:, HALF:], -sine[:, HALF:]], 1)
    imag = np.concatenate([sine[:, :HALF], cosine[:, :HALF], sine[:, HALF:], cosine[:, HALF:]], 1)
    turn = np.concatenate([real, imag], axis=0) / float(GRID**3)
    turn = np.pad(turn, ((0, 0), (0, ROWS - turn.shape[1]))).astype(np.float32)

    def columns(value):
        high = lax.reduce_precision(value, 8, 7)
        return jnp.concatenate([high, value - high, high], axis=1).astype(jnp.bfloat16)

    atoms = y_hat.shape[0]
    piece = (ROWS, LANES)
    half = chunks // 2
    return pl.pallas_call(
        functools.partial(window_kernel, lax.axis_size("rec")),
        out_shape=jax.ShapeDtypeStruct((2 * GRID, width), jnp.float32),
        in_specs=[pl.BlockSpec(memory_space=pltpu.VMEM)] * 7,
        out_specs=pl.BlockSpec(memory_space=pltpu.VMEM),
        scratch_shapes=[
            pltpu.VMEM((chunks,) + piece, jnp.float32),
            pltpu.VMEM((half,) + piece, jnp.float32),
            pltpu.VMEM((half,) + piece, jnp.float32),
            pltpu.VMEM((half,) + piece, jnp.float32),
            pltpu.VMEM((chunks,) + piece, jnp.float32),
            pltpu.VMEM((chunks,) + piece, jnp.float32),
            pltpu.VMEM((atoms, 2 * LANES), jnp.float32),
            pltpu.VMEM((ROWS, 2 * atoms), jnp.bfloat16),
            pltpu.VMEM((ROWS, 2 * atoms), jnp.bfloat16),
        ]
        + [pltpu.SemaphoreType.DMA((half,))] * 6,
        compiler_params=pltpu.CompilerParams(
            collective_id=0, has_side_effects=True, vmem_limit_bytes=40 * 1024 * 1024
        ),
    )(
        folded, left, columns(y_hat), columns(z_hat),
        jnp.asarray(y_table), jnp.asarray(z_table), jnp.asarray(turn),
    )


def hats_of(record, rotations, ligand_coords, atom_types, channel_weights):
    table_rows = rotations.shape[0]
    picks = (record[:, None] == jnp.arange(table_rows, dtype=jnp.int32)[None, :]).astype(
        jnp.float32
    )
    matrix = jnp.dot(picks, rotations.reshape(table_rows, 9), precision=HIGHEST)[0]
    kinds = channel_weights.shape[0]
    type_hot = (atom_types[:, None] == jnp.arange(kinds, dtype=jnp.int32)[None, :]).astype(
        jnp.float32
    )
    weights = jnp.dot(type_hot, channel_weights, precision=HIGHEST)
    coords = ligand_coords.astype(jnp.float32) * (1.0 / 256.0)
    places = [
        0.5 * GRID
        + (
            matrix[3 * row] * coords[0]
            + matrix[3 * row + 1] * coords[1]
            + matrix[3 * row + 2] * coords[2]
        )
        for row in range(3)
    ]
    cells = jnp.arange(GRID, dtype=jnp.float32)
    odd = (jnp.arange(GRID, dtype=jnp.int32) * lax.axis_index("fft")) % 2
    y_hat = hat_rows(places[1], cells) * weights * (1.0 - 2.0 * odd.astype(jnp.float32))
    z_hat = hat_rows(places[2], cells)
    cosine, sine = host_waves(np.arange(HALF + 1), np.arange(GRID))
    none = np.zeros((6, GRID))
    meet_re = np.concatenate([cosine[:HALF], sine[:HALF], cosine[HALF:], sine[HALF:], none], 0)
    meet_im = np.concatenate([-sine[:HALF], cosine[:HALF], -sine[HALF:], cosine[HALF:], none], 0)
    table = jnp.asarray(np.stack([meet_re, meet_im], axis=1).reshape(2 * ROWS, GRID), jnp.float32)
    x_hat = jnp.maximum(0.0, 1.0 - jnp.abs(places[0][None, :] - cells[:, None]))
    left = jnp.dot(table, x_hat, precision=HIGHEST).reshape(ROWS, 2 * x_hat.shape[1])
    return left, y_hat, z_hat


def body(record_ids, rotations, ligand_coords, atom_types, channel_weights, receptor_spectra):
    width = receptor_spectra.shape[-1]
    slab = GRID // lax.axis_size("fft")
    record = from_behind(record_ids, "rec", 2)
    folded = fold(receptor_spectra[0, 0], width)
    folded = jnp.concatenate(
        [
            folded[:, :HALF].reshape(GRID, width),
            folded[:, HALF],
            jnp.zeros((ROWS - GRID - 2, width), jnp.float32),
        ],
        axis=0,
    )
    left, y_hat, z_hat = hats_of(record, rotations, ligand_coords, atom_types, channel_weights)
    turned = turned_product(folded, left, y_hat, z_hat, width).reshape(1, 2, GRID, width)
    index = jnp.arange(GRID, dtype=jnp.int32)
    halves = lax.all_to_all(turned, "fft", split_axis=2, concat_axis=3, tiled=True)
    volume = halves.reshape(2, slab, GRID, GRID)
    cosine, sine = waves(index, index)
    z_turn = jnp.stack([cosine, -sine])

    def scores(places):
        y_cos, y_sin = waves(index, places)
        y_turn = jnp.stack([jnp.stack([y_cos, -y_sin]), jnp.stack([y_sin, y_cos])])
        in_y = jnp.einsum("dcky,cxkz->dxyz", y_turn, volume, precision=HIGH)
        part = jnp.einsum("dxyz,dzt->xyt", in_y, z_turn, precision=HIGH)
        return part.reshape(1, slab, places.shape[0] * GRID)

    count = lax.axis_size("chan")
    if count != 2:
        return lax.psum_scatter(scores(index), "chan", scatter_dimension=2, tiled=True)
    near = lax.axis_index("chan") * HALF + jnp.arange(HALF, dtype=jnp.int32)
    far = (near + HALF) % GRID
    arrived = from_behind(scores(far), "chan", 1)
    return scores(near) + arrived


def solution(mesh):
    in_specs = (
        P(("grp", "rec")),
        P(),
        P(None, "grp"),
        P("grp"),
        P(None, "chan"),
        P("rec", "chan", None, None, "fft"),
    )
    out_specs = P(("grp", "rec"), "fft", "chan")
    return jax.shard_map(body, mesh=mesh, in_specs=in_specs, out_specs=out_specs, check_vma=False)
```

```python
import math

import functools

import jax
import jax.numpy as jnp
import numpy as np
from jax import lax
from jax.experimental import pallas as pl
from jax.experimental.pallas import tpu as pltpu
from jax.sharding import PartitionSpec as P

GRID = 64
HALF = GRID // 2
HIGHEST = lax.Precision.HIGHEST
HIGH = lax.Precision.HIGH


def from_behind(value, axis, steps):
    count = lax.axis_size(axis)
    pairs = [(source, (source + steps) % count) for source in range(count)]
    return lax.ppermute(value, axis, pairs)


def waves(rows, columns):
    phase = rows[:, None] * columns[None, :] % GRID
    angle = phase.astype(jnp.float32) * (2.0 * math.pi / GRID)
    return jnp.cos(angle), jnp.sin(angle)


def host_waves(rows, columns):
    angle = (np.outer(rows, columns) % GRID) * (2.0 * np.pi / GRID)
    return np.cos(angle), np.sin(angle)


def tripled(table):
    table = table.astype(np.float32)
    high = table.astype(jnp.bfloat16)
    low = (table - high.astype(np.float32)).astype(jnp.bfloat16)
    return np.concatenate([high, high, low], axis=0)


ROWS = 72
LANES = 256


def split(value):
    high = value.astype(jnp.bfloat16)
    return high, (value - high.astype(jnp.float32)).astype(jnp.bfloat16)


def dot(left, right):
    return jnp.dot(left, right, preferred_element_type=jnp.float32)


def window_kernel(
    count, s_ref, flip_ref, rows_ref, l_ref, y_ref, z_ref, yt_ref, zt_ref, turn_ref, out_ref,
    source, own, first, pair, second, win, lig, z_wave, l_high, l_low,
    send0, recv0, send1, recv1, send2, recv2, send3, recv3,
):
    grp = lax.axis_index("grp")
    rec = lax.axis_index("rec")
    after = lax.rem(rec + 1, count)
    before = lax.rem(rec + count - 1, count)
    chunks = win.shape[0]
    mine = chunks // 2
    barrier = pltpu.get_barrier_semaphore()
    fft = lax.axis_index("fft")
    for target in ({"rec": after}, {"rec": before}, {"grp": 1 - grp}, {"fft": 1 - fft}):
        pl.semaphore_signal(
            barrier, inc=1, device_id=target, device_id_type=pl.DeviceIdType.MESH
        )
    width = s_ref.shape[2]
    for part in range(2):
        source[part * HALF : (part + 1) * HALF, width:] = s_ref[part, HALF:, 0:128]
    pl.semaphore_wait(barrier, 4)
    base = grp * mine

    def remote(source, target, send, recv, device):
        return pltpu.make_async_remote_copy(
            src_ref=source, dst_ref=target, send_sem=send, recv_sem=recv,
            device_id=device, device_id_type=pl.DeviceIdType.MESH,
        )

    ones = [
        remote(own.at[c], first.at[c], send1.at[c], recv1.at[c], {"rec": after})
        for c in range(mine)
    ]
    twos = [
        remote(pair.at[c], second.at[c], send2.at[c], recv2.at[c], {"rec": after})
        for c in range(mine)
    ]
    threes = [
        remote(win.at[base + c], win.at[base + c], send3.at[c], recv3.at[c], {"grp": 1 - grp})
        for c in range(mine)
    ]
    reach = pl.ds(pl.multiple_of((1 - grp) * (width // 2 - 128), 128), width // 2 + 128)
    zeros = [
        remote(
            s_ref.at[part, pl.ds(HALF, HALF), reach],
            source.at[pl.ds(part * HALF, HALF), reach],
            send0.at[part], recv0.at[part], {"fft": 1 - fft},
        )
        for part in range(2)
    ]
    for copy in zeros:
        copy.start()

    z_wave[...] = dot(z_ref[...], zt_ref[...])
    high, low = split(l_ref[...])
    l_high[...] = high
    l_low[...] = low

    def fold(c):
        chunk = base + c
        window = pl.ds(pl.multiple_of((2 * (chunks - 1) - 2 * chunk) * 128, 128), 384)
        high, low = split(source[:, window])
        flipped = dot(jnp.concatenate([high, low], axis=0), flip_ref[...])
        mirrored = dot(rows_ref[...], flipped.astype(jnp.bfloat16))
        lanes = pl.ds(pl.multiple_of(chunk * LANES, LANES), LANES)
        own[c, 0:32] = s_ref[0, 0:32, lanes] + mirrored[0:32]
        own[c, 32:64] = s_ref[1, 0:32, lanes] + mirrored[32:64]
        row = lax.broadcasted_iota(jnp.int32, (8, LANES), 0)
        re, im = s_ref[0, 32:40, lanes][0:1], s_ref[1, 32:40, lanes][0:1]
        own[c, 64:72] = jnp.where(row == 0, re, jnp.where(row == 1, im, 0.0))

    def ligand(chunk):
        y_wave = dot(y_ref[...], yt_ref[chunk])
        y_re, y_im = y_wave[:, :LANES], y_wave[:, LANES:]
        z_re, z_im = z_wave[:, :LANES], z_wave[:, LANES:]
        re_high, re_low = split(y_re * z_re - y_im * z_im)
        im_high, im_low = split(y_re * z_im + y_im * z_re)
        v_high = jnp.concatenate([re_high, im_high], axis=0)
        v_low = jnp.concatenate([re_low, im_low], axis=0)
        lig[chunk] = (
            dot(l_high[...], v_high) + dot(l_low[...], v_high) + dot(l_high[...], v_low)
        )

    t_high, t_low = split(turn_ref[...])

    def product(chunk):
        l_re, l_im = lig[chunk, 0:32], lig[chunk, 32:64]
        w_re, w_im = win[chunk, 0:32], win[chunk, 32:64]
        tail_l, tail_w = lig[chunk, 64:72], win[chunk, 64:72]
        a, b = tail_l[0:1], tail_l[1:2]
        c, d = tail_w[0:1], tail_w[1:2]
        row = lax.broadcasted_iota(jnp.int32, (8, LANES), 0)
        tail = jnp.where(row == 0, a * c - b * d, jnp.where(row == 1, a * d + b * c, 0.0))
        whole = jnp.concatenate([l_re * w_re - l_im * w_im, l_re * w_im + l_im * w_re, tail], axis=0)
        p_high, p_low = split(whole)
        lanes = pl.ds(pl.multiple_of(chunk * LANES, LANES), LANES)
        out_ref[:, lanes] = dot(t_high, p_high) + dot(t_low, p_high) + dot(t_high, p_low)

    ligand(0)
    for copy in zeros:
        copy.wait_recv()
    for c in range(mine):
        fold(c)
        ones[c].start()
    ligand(1)
    ligand(2)
    for c in range(mine):
        ones[c].wait_recv()
        pair[c] = own[c] + first[c]
        twos[c].start()
        ligand(3 + c)
    ligand(7)
    for c in range(mine):
        twos[c].wait_recv()
        win[base + c] = own[c] + second[c]
        threes[c].start()
        product(base + c)
    for c in range(mine):
        threes[c].wait_recv()
        product((1 - grp) * mine + c)
    for copy in zeros + ones + twos + threes:
        copy.wait_send()


def turned_product(receptor, left, y_hat, z_hat, width):
    index = np.arange(GRID)
    chunks = width // LANES
    lane = np.arange(width)
    cosine, sine = host_waves(index, lane // GRID)
    y_table = np.stack(
        [
            tripled(
                np.concatenate(
                    [t[:, c * LANES : (c + 1) * LANES] for t in (cosine, sine)], axis=1
                )
            )
            for c in range(chunks)
        ]
    )
    z_table = tripled(np.concatenate(host_waves(index, lane[:LANES] % GRID), axis=1))
    cosine, sine = host_waves(index, np.arange(HALF + 1))
    real = np.concatenate([cosine[:, :HALF], -sine[:, :HALF], cosine[:, HALF:], -sine[:, HALF:]], 1)
    imag = np.concatenate([sine[:, :HALF], cosine[:, :HALF], sine[:, HALF:], cosine[:, HALF:]], 1)
    turn = np.concatenate([real, imag], axis=0) / float(GRID**3)
    turn = np.pad(turn, ((0, 0), (0, ROWS - turn.shape[1]))).astype(np.float32)

    def columns(value):
        high = lax.reduce_precision(value, 8, 7)
        return jnp.concatenate([high, value - high, high], axis=1).astype(jnp.bfloat16)

    flip = np.zeros((384, LANES), np.float32)
    for m in range(LANES // GRID):
        for kz in range(GRID):
            flip[(4 - m) * GRID + (-kz) % GRID, m * GRID + kz] = 1.0
    flip = flip.astype(jnp.bfloat16)
    rows = np.zeros((2 * HALF, 2 * HALF), np.float32)
    for kx in range(1, HALF):
        rows[kx, HALF - kx] = 1.0
        rows[HALF + kx, 2 * HALF - kx] = -1.0
    rows = np.concatenate([rows, rows], axis=1).astype(jnp.bfloat16)
    atoms = y_hat.shape[0]
    piece = (ROWS, LANES)
    half = chunks // 2
    return pl.pallas_call(
        functools.partial(window_kernel, lax.axis_size("rec")),
        out_shape=jax.ShapeDtypeStruct((2 * GRID, width), jnp.float32),
        in_specs=[pl.BlockSpec(memory_space=pltpu.VMEM)] * 9,
        out_specs=pl.BlockSpec(memory_space=pltpu.VMEM),
        scratch_shapes=[
            pltpu.VMEM((2 * HALF, width + 128), jnp.float32),
            pltpu.VMEM((half,) + piece, jnp.float32),
            pltpu.VMEM((half,) + piece, jnp.float32),
            pltpu.VMEM((half,) + piece, jnp.float32),
            pltpu.VMEM((half,) + piece, jnp.float32),
            pltpu.VMEM((chunks,) + piece, jnp.float32),
            pltpu.VMEM((chunks,) + piece, jnp.float32),
            pltpu.VMEM((atoms, 2 * LANES), jnp.float32),
            pltpu.VMEM((ROWS, 2 * atoms), jnp.bfloat16),
            pltpu.VMEM((ROWS, 2 * atoms), jnp.bfloat16),
        ]
        + [pltpu.SemaphoreType.DMA((2,))] * 2
        + [pltpu.SemaphoreType.DMA((half,))] * 6,
        compiler_params=pltpu.CompilerParams(
            collective_id=0, has_side_effects=True, vmem_limit_bytes=40 * 1024 * 1024
        ),
    )(
        receptor, jnp.asarray(flip), jnp.asarray(rows), left, columns(y_hat), columns(z_hat),
        jnp.asarray(y_table), jnp.asarray(z_table), jnp.asarray(turn),
    )


def hats_of(record, rotations, ligand_coords, atom_types, channel_weights):
    table_rows = rotations.shape[0]
    picks = (record[:, None] == jnp.arange(table_rows, dtype=jnp.int32)[None, :]).astype(
        jnp.float32
    )
    matrix = jnp.dot(picks, rotations.reshape(table_rows, 9), precision=HIGHEST)[0]
    kinds = channel_weights.shape[0]
    type_hot = (atom_types[:, None] == jnp.arange(kinds, dtype=jnp.int32)[None, :]).astype(
        jnp.float32
    )
    weights = jnp.dot(
        type_hot, jnp.broadcast_to(channel_weights, (kinds, GRID)), precision=HIGHEST
    )
    coords = ligand_coords.astype(jnp.float32) * (1.0 / 256.0)
    matrix = matrix.reshape(3, 3)
    center = 0.5 * GRID
    cells = jnp.arange(GRID, dtype=jnp.float32)
    offset = center - jnp.concatenate([cells, cells])
    spread = jnp.repeat(matrix[1:].T, GRID, axis=1)
    hats = jnp.maximum(
        0.0, 1.0 - jnp.abs(jnp.dot(coords.T, spread, precision=HIGHEST) + offset[None, :])
    )
    x_places = jnp.dot(jnp.broadcast_to(matrix[0], (GRID, 3)), coords, precision=HIGHEST)
    x_hat = jnp.maximum(0.0, 1.0 - jnp.abs(x_places + (center - cells)[:, None]))
    odd = (jnp.arange(GRID, dtype=jnp.int32) * lax.axis_index("fft")) % 2
    y_hat = hats[:, :GRID] * weights * (1.0 - 2.0 * odd.astype(jnp.float32))
    z_hat = hats[:, GRID:]
    cosine, sine = host_waves(np.arange(HALF + 1), np.arange(GRID))
    none = np.zeros((6, GRID))
    meet_re = np.concatenate([cosine[:HALF], sine[:HALF], cosine[HALF:], sine[HALF:], none], 0)
    meet_im = np.concatenate([-sine[:HALF], cosine[:HALF], -sine[HALF:], cosine[HALF:], none], 0)
    table = jnp.asarray(np.stack([meet_re, meet_im], axis=1).reshape(2 * ROWS, GRID), jnp.float32)
    left = jnp.dot(table, x_hat, precision=HIGHEST).reshape(ROWS, 2 * x_hat.shape[1])
    return left, y_hat, z_hat


def body(record_ids, rotations, ligand_coords, atom_types, channel_weights, receptor_spectra):
    width = receptor_spectra.shape[-1]
    slab = GRID // lax.axis_size("fft")
    record = from_behind(record_ids, "rec", 2)
    left, y_hat, z_hat = hats_of(record, rotations, ligand_coords, atom_types, channel_weights)
    turned = turned_product(receptor_spectra[0, 0], left, y_hat, z_hat, width).reshape(1, 2, GRID, width)
    index = jnp.arange(GRID, dtype=jnp.int32)
    halves = lax.all_to_all(turned, "fft", split_axis=2, concat_axis=3, tiled=True)
    volume = halves.reshape(2, slab, GRID, GRID)
    cosine, sine = waves(index, index)
    z_turn = jnp.stack([cosine, -sine])

    def scores(places):
        y_cos, y_sin = waves(index, places)
        y_turn = jnp.stack([jnp.stack([y_cos, -y_sin]), jnp.stack([y_sin, y_cos])])
        in_y = jnp.einsum("dcky,cxkz->dxyz", y_turn, volume, precision=HIGH)
        part = jnp.einsum("dxyz,dzt->xyt", in_y, z_turn, precision=HIGH)
        return part.reshape(1, slab, places.shape[0] * GRID)

    count = lax.axis_size("chan")
    if count != 2:
        return lax.psum_scatter(scores(index), "chan", scatter_dimension=2, tiled=True)
    near = lax.axis_index("chan") * HALF + jnp.arange(HALF, dtype=jnp.int32)
    far = (near + HALF) % GRID
    arrived = from_behind(scores(far), "chan", 1)
    return scores(near) + arrived


def solution(mesh):
    in_specs = (
        P(("grp", "rec")),
        P(),
        P(None, "grp"),
        P("grp"),
        P(None, "chan"),
        P("rec", "chan", None, None, "fft"),
    )
    out_specs = P(("grp", "rec"), "fft", "chan")
    return jax.shard_map(body, mesh=mesh, in_specs=in_specs, out_specs=out_specs, check_vma=False)
```

```python
import math

import functools

import jax
import jax.numpy as jnp
import numpy as np
from jax import lax
from jax.experimental import pallas as pl
from jax.experimental.pallas import tpu as pltpu
from jax.sharding import PartitionSpec as P

GRID = 64
HALF = GRID // 2
HIGHEST = lax.Precision.HIGHEST
HIGH = lax.Precision.HIGH


def from_behind(value, axis, steps):
    count = lax.axis_size(axis)
    pairs = [(source, (source + steps) % count) for source in range(count)]
    return lax.ppermute(value, axis, pairs)


def host_waves(rows, columns):
    angle = (np.outer(rows, columns) % GRID) * (2.0 * np.pi / GRID)
    return np.cos(angle), np.sin(angle)


def tripled(table):
    table = table.astype(np.float32)
    high = table.astype(jnp.bfloat16)
    low = (table - high.astype(np.float32)).astype(jnp.bfloat16)
    return np.concatenate([high, high, low, np.zeros_like(low)], axis=0)


ROWS = 72
LANES = 256


def split(value):
    high = value.astype(jnp.bfloat16)
    return high, (value - high.astype(jnp.float32)).astype(jnp.bfloat16)


def dot(left, right):
    return jnp.dot(left, right, preferred_element_type=jnp.float32)


def window_kernel(
    count, s_ref, flip_ref, rows_ref, xt_ref, x_ref, hat_ref, weight_ref, yt_ref, zt_ref, turn_ref, out_ref,
    source, own, first, pair, second, win, lig, y_cols, z_wave, l_high, l_low,
    send0, recv0, send1, recv1, send2, recv2, send3, recv3,
):
    grp = lax.axis_index("grp")
    rec = lax.axis_index("rec")
    after = lax.rem(rec + 1, count)
    before = lax.rem(rec + count - 1, count)
    chunks = win.shape[0]
    mine = chunks // 2
    barrier = pltpu.get_barrier_semaphore()
    fft = lax.axis_index("fft")
    for target in ({"rec": after}, {"rec": before}, {"grp": 1 - grp}, {"fft": 1 - fft}):
        pl.semaphore_signal(
            barrier, inc=1, device_id=target, device_id_type=pl.DeviceIdType.MESH
        )
    width = s_ref.shape[2]
    for part in range(2):
        source[part * HALF : (part + 1) * HALF, width:] = s_ref[part, HALF:, 0:128]
    pl.semaphore_wait(barrier, 4)
    base = grp * mine

    def remote(source, target, send, recv, device):
        return pltpu.make_async_remote_copy(
            src_ref=source, dst_ref=target, send_sem=send, recv_sem=recv,
            device_id=device, device_id_type=pl.DeviceIdType.MESH,
        )

    ones = [
        remote(own.at[c], first.at[c], send1.at[c], recv1.at[c], {"rec": after})
        for c in range(mine)
    ]
    twos = [
        remote(pair.at[c], second.at[c], send2.at[c], recv2.at[c], {"rec": after})
        for c in range(mine)
    ]
    threes = [
        remote(win.at[base + c], win.at[base + c], send3.at[c], recv3.at[c], {"grp": 1 - grp})
        for c in range(mine)
    ]
    reach = pl.ds(pl.multiple_of((1 - grp) * (width // 2 - 128), 128), width // 2 + 128)
    zeros = [
        remote(
            s_ref.at[part, pl.ds(HALF, HALF), reach],
            source.at[pl.ds(part * HALF, HALF), reach],
            send0.at[part], recv0.at[part], {"fft": 1 - fft},
        )
        for part in range(2)
    ]
    for copy in zeros:
        copy.start()

    def columns(value):
        high = value.astype(jnp.bfloat16)
        rounded = high.astype(jnp.float32)
        lane = lax.broadcasted_iota(jnp.int32, value.shape, 1)
        mixed = jnp.where(lane < GRID, rounded, value - rounded).astype(jnp.bfloat16)
        return jnp.concatenate([mixed, high], axis=1)

    y_cols[...] = columns(hat_ref[:, 0:128] * weight_ref[...])
    z_wave[...] = dot(columns(hat_ref[:, 128:256]), zt_ref[...])
    x_high, x_low = split(x_ref[...])
    atoms = x_ref.shape[1]
    for part in range(2):
        xt_high, xt_low = split(xt_ref[part])
        left = dot(xt_high, x_high) + dot(xt_low, x_high) + dot(xt_high, x_low)
        high, low = split(left)
        l_high[:, part * atoms : (part + 1) * atoms] = high
        l_low[:, part * atoms : (part + 1) * atoms] = low

    def fold(c):
        chunk = base + c
        window = pl.ds(pl.multiple_of((2 * (chunks - 1) - 2 * chunk) * 128, 128), 384)
        high, low = split(source[:, window])
        flipped = dot(jnp.concatenate([high, low], axis=0), flip_ref[...])
        mirrored = dot(rows_ref[...], flipped.astype(jnp.bfloat16))
        lanes = pl.ds(pl.multiple_of(chunk * LANES, LANES), LANES)
        own[c, 0:32] = s_ref[0, 0:32, lanes] + mirrored[0:32]
        own[c, 32:64] = s_ref[1, 0:32, lanes] + mirrored[32:64]
        row = lax.broadcasted_iota(jnp.int32, (8, LANES), 0)
        re, im = s_ref[0, 32:40, lanes][0:1], s_ref[1, 32:40, lanes][0:1]
        own[c, 64:72] = jnp.where(row == 0, re, jnp.where(row == 1, im, 0.0))

    def ligand(chunk):
        y_wave = dot(y_cols[...], yt_ref[chunk])
        y_re, y_im = y_wave[:, :LANES], y_wave[:, LANES:]
        z_re, z_im = z_wave[:, :LANES], z_wave[:, LANES:]
        re_high, re_low = split(y_re * z_re - y_im * z_im)
        im_high, im_low = split(y_re * z_im + y_im * z_re)
        v_high = jnp.concatenate([re_high, im_high], axis=0)
        v_low = jnp.concatenate([re_low, im_low], axis=0)
        lig[chunk] = (
            dot(l_high[...], v_high) + dot(l_low[...], v_high) + dot(l_high[...], v_low)
        )

    t_high, t_low = split(turn_ref[...])

    def product(chunk):
        l_re, l_im = lig[chunk, 0:32], lig[chunk, 32:64]
        w_re, w_im = win[chunk, 0:32], win[chunk, 32:64]
        tail_l, tail_w = lig[chunk, 64:72], win[chunk, 64:72]
        a, b = tail_l[0:1], tail_l[1:2]
        c, d = tail_w[0:1], tail_w[1:2]
        row = lax.broadcasted_iota(jnp.int32, (8, LANES), 0)
        tail = jnp.where(row == 0, a * c - b * d, jnp.where(row == 1, a * d + b * c, 0.0))
        whole = jnp.concatenate([l_re * w_re - l_im * w_im, l_re * w_im + l_im * w_re, tail], axis=0)
        p_high, p_low = split(whole)
        lanes = pl.ds(pl.multiple_of(chunk * LANES, LANES), LANES)
        out_ref[:, lanes] = dot(t_high, p_high) + dot(t_low, p_high) + dot(t_high, p_low)

    ligand(0)
    for copy in zeros:
        copy.wait_recv()
    for c in range(mine):
        fold(c)
        ones[c].start()
    ligand(1)
    ligand(2)
    for c in range(mine):
        ones[c].wait_recv()
        pair[c] = own[c] + first[c]
        twos[c].start()
        ligand(3 + c)
    ligand(7)
    for c in range(mine):
        twos[c].wait_recv()
        win[base + c] = own[c] + second[c]
        threes[c].start()
        product(base + c)
    for c in range(mine):
        threes[c].wait_recv()
        product((1 - grp) * mine + c)
    for copy in zeros + ones + twos + threes:
        copy.wait_send()


def turned_product(receptor, table, x_hat, hats, weights, width):
    index = np.arange(GRID)
    chunks = width // LANES
    lane = np.arange(width)
    cosine, sine = host_waves(index, lane // GRID)
    y_table = np.stack(
        [
            tripled(
                np.concatenate(
                    [t[:, c * LANES : (c + 1) * LANES] for t in (cosine, sine)], axis=1
                )
            )
            for c in range(chunks)
        ]
    )
    z_table = tripled(np.concatenate(host_waves(index, lane[:LANES] % GRID), axis=1))
    cosine, sine = host_waves(index, np.arange(HALF + 1))
    real = np.concatenate([cosine[:, :HALF], -sine[:, :HALF], cosine[:, HALF:], -sine[:, HALF:]], 1)
    imag = np.concatenate([sine[:, :HALF], cosine[:, :HALF], sine[:, HALF:], cosine[:, HALF:]], 1)
    turn = np.concatenate([real, imag], axis=0) / float(GRID**3)
    turn = np.pad(turn, ((0, 0), (0, ROWS - turn.shape[1]))).astype(np.float32)

    flip = np.zeros((384, LANES), np.float32)
    for m in range(LANES // GRID):
        for kz in range(GRID):
            flip[(4 - m) * GRID + (-kz) % GRID, m * GRID + kz] = 1.0
    flip = flip.astype(jnp.bfloat16)
    rows = np.zeros((2 * HALF, 2 * HALF), np.float32)
    for kx in range(1, HALF):
        rows[kx, HALF - kx] = 1.0
        rows[HALF + kx, 2 * HALF - kx] = -1.0
    rows = np.concatenate([rows, rows], axis=1).astype(jnp.bfloat16)
    atoms = hats.shape[0]
    piece = (ROWS, LANES)
    half = chunks // 2
    return pl.pallas_call(
        functools.partial(window_kernel, lax.axis_size("rec")),
        out_shape=jax.ShapeDtypeStruct((2 * GRID, width), jnp.float32),
        in_specs=[pl.BlockSpec(memory_space=pltpu.VMEM)] * 10,
        out_specs=pl.BlockSpec(memory_space=pltpu.VMEM),
        scratch_shapes=[
            pltpu.VMEM((2 * HALF, width + 128), jnp.float32),
            pltpu.VMEM((half,) + piece, jnp.float32),
            pltpu.VMEM((half,) + piece, jnp.float32),
            pltpu.VMEM((half,) + piece, jnp.float32),
            pltpu.VMEM((half,) + piece, jnp.float32),
            pltpu.VMEM((chunks,) + piece, jnp.float32),
            pltpu.VMEM((chunks,) + piece, jnp.float32),
            pltpu.VMEM((atoms, 4 * GRID), jnp.bfloat16),
            pltpu.VMEM((atoms, 2 * LANES), jnp.float32),
            pltpu.VMEM((ROWS, 2 * atoms), jnp.bfloat16),
            pltpu.VMEM((ROWS, 2 * atoms), jnp.bfloat16),
        ]
        + [pltpu.SemaphoreType.DMA((2,))] * 2
        + [pltpu.SemaphoreType.DMA((half,))] * 6,
        compiler_params=pltpu.CompilerParams(
            collective_id=0, has_side_effects=True, vmem_limit_bytes=40 * 1024 * 1024
        ),
    )(
        receptor, jnp.asarray(flip), jnp.asarray(rows), table, x_hat, hats, weights,
        jnp.asarray(y_table), jnp.asarray(z_table), jnp.asarray(turn),
    )


def hats_of(record, rotations, ligand_coords, atom_types, channel_weights):
    table_rows = rotations.shape[0]
    picks = (record[:, None] == jnp.arange(table_rows, dtype=jnp.int32)[None, :]).astype(
        jnp.float32
    )
    matrix = jnp.dot(picks, rotations.reshape(table_rows, 9), precision=HIGHEST)[0]
    kinds = channel_weights.shape[0]
    type_hot = (atom_types[:, None] == jnp.arange(kinds, dtype=jnp.int32)[None, :]).astype(
        jnp.float32
    )
    odd = (jnp.arange(2 * GRID, dtype=jnp.int32) * lax.axis_index("fft")) % 2
    sign = 1.0 - 2.0 * odd.astype(jnp.float32)[None, :]
    weights = jnp.dot(
        type_hot, jnp.broadcast_to(channel_weights, (kinds, 2 * GRID)) * sign, precision=HIGHEST
    )
    coords = ligand_coords.astype(jnp.float32) * (1.0 / 256.0)
    matrix = matrix.reshape(3, 3)
    center = 0.5 * GRID
    cells = jnp.arange(GRID, dtype=jnp.float32)
    offset = center - jnp.concatenate([cells] * 4)
    spread = jnp.repeat(matrix[1:].T, 2 * GRID, axis=1)
    hats = jnp.maximum(
        0.0, 1.0 - jnp.abs(jnp.dot(coords.T, spread, precision=HIGHEST) + offset[None, :])
    )
    x_places = jnp.dot(jnp.broadcast_to(matrix[0], (GRID, 3)), coords, precision=HIGHEST)
    x_hat = jnp.maximum(0.0, 1.0 - jnp.abs(x_places + (center - cells)[:, None]))
    cosine, sine = host_waves(np.arange(HALF + 1), np.arange(GRID))
    none = np.zeros((6, GRID))
    meet_re = np.concatenate([cosine[:HALF], sine[:HALF], cosine[HALF:], sine[HALF:], none], 0)
    meet_im = np.concatenate([-sine[:HALF], cosine[:HALF], -sine[HALF:], cosine[HALF:], none], 0)
    table = jnp.asarray(np.stack([meet_re, meet_im]), jnp.float32)
    return table, x_hat, hats, weights


def body(record_ids, rotations, ligand_coords, atom_types, channel_weights, receptor_spectra):
    width = receptor_spectra.shape[-1]
    slab = GRID // lax.axis_size("fft")
    record = from_behind(record_ids, "rec", 2)
    parts = hats_of(record, rotations, ligand_coords, atom_types, channel_weights)
    turned = turned_product(receptor_spectra[0, 0], *parts, width).reshape(1, 2, GRID, width)
    index = np.arange(GRID)
    halves = lax.all_to_all(turned, "fft", split_axis=2, concat_axis=3, tiled=True)
    volume = halves.reshape(2, slab, GRID, GRID)
    cosine, sine = host_waves(index, index)
    z_turn = jnp.asarray(np.stack([cosine, -sine]), jnp.float32)
    y_all = np.stack([np.stack([cosine, -sine]), np.stack([sine, cosine])])

    def scores(y_turn):
        in_y = jnp.einsum("dcky,cxkz->dxyz", y_turn, volume, precision=HIGH)
        part = jnp.einsum("dxyz,dzt->xyt", in_y, z_turn, precision=HIGH)
        return part.reshape(1, slab, y_turn.shape[3] * GRID)

    count = lax.axis_size("chan")
    if count != 2:
        return lax.psum_scatter(scores(jnp.asarray(y_all, jnp.float32)), "chan", scatter_dimension=2, tiled=True)
    halves_y = jnp.asarray(np.stack([y_all[..., :HALF], y_all[..., HALF:]]), jnp.float32)
    me = lax.axis_index("chan")
    near = lax.dynamic_index_in_dim(halves_y, me, 0, keepdims=False)
    far = lax.dynamic_index_in_dim(halves_y, 1 - me, 0, keepdims=False)
    arrived = from_behind(scores(far), "chan", 1)
    return scores(near) + arrived


def solution(mesh):
    in_specs = (
        P(("grp", "rec")),
        P(),
        P(None, "grp"),
        P("grp"),
        P(None, "chan"),
        P("rec", "chan", None, None, "fft"),
    )
    out_specs = P(("grp", "rec"), "fft", "chan")
    return jax.shard_map(body, mesh=mesh, in_specs=in_specs, out_specs=out_specs, check_vma=False)
```

```python
import math

import functools

import jax
import jax.numpy as jnp
import numpy as np
from jax import lax
from jax.experimental import pallas as pl
from jax.experimental.pallas import tpu as pltpu
from jax.sharding import PartitionSpec as P

GRID = 64
HALF = GRID // 2
HIGHEST = lax.Precision.HIGHEST
HIGH = lax.Precision.HIGH


def from_behind(value, axis, steps):
    count = lax.axis_size(axis)
    pairs = [(source, (source + steps) % count) for source in range(count)]
    return lax.ppermute(value, axis, pairs)


def host_waves(rows, columns):
    angle = (np.outer(rows, columns) % GRID) * (2.0 * np.pi / GRID)
    return np.cos(angle), np.sin(angle)


def tripled(table):
    table = table.astype(np.float32)
    high = table.astype(jnp.bfloat16)
    low = (table - high.astype(np.float32)).astype(jnp.bfloat16)
    return np.concatenate([high, high, low, np.zeros_like(low)], axis=0)


ROWS = 72
LANES = 256


def split(value):
    high = value.astype(jnp.bfloat16)
    return high, (value - high.astype(jnp.float32)).astype(jnp.bfloat16)


def dot(left, right):
    return jnp.dot(left, right, preferred_element_type=jnp.float32)


def window_kernel(
    count, s_ref, yt_ref, ft_ref, x_ref, hat_ref, weight_ref, out_ref,
    source, own, first, pair, second, win, lig, y_cols, z_wave, l_high, l_low,
    send0, recv0, send1, recv1, send2, recv2, send3, recv3,
):
    grp = lax.axis_index("grp")
    rec = lax.axis_index("rec")
    after = lax.rem(rec + 1, count)
    before = lax.rem(rec + count - 1, count)
    chunks = win.shape[0]
    mine = chunks // 2
    barrier = pltpu.get_barrier_semaphore()
    fft = lax.axis_index("fft")
    for target in ({"rec": after}, {"rec": before}, {"grp": 1 - grp}, {"fft": 1 - fft}):
        pl.semaphore_signal(
            barrier, inc=1, device_id=target, device_id_type=pl.DeviceIdType.MESH
        )
    width = s_ref.shape[2]
    for part in range(2):
        source[part * HALF : (part + 1) * HALF, width:] = s_ref[part, HALF:, 0:128]
    pl.semaphore_wait(barrier, 4)
    base = grp * mine

    def remote(source, target, send, recv, device):
        return pltpu.make_async_remote_copy(
            src_ref=source, dst_ref=target, send_sem=send, recv_sem=recv,
            device_id=device, device_id_type=pl.DeviceIdType.MESH,
        )

    ones = [
        remote(own.at[c], first.at[c], send1.at[c], recv1.at[c], {"rec": after})
        for c in range(mine)
    ]
    twos = [
        remote(pair.at[c], second.at[c], send2.at[c], recv2.at[c], {"rec": after})
        for c in range(mine)
    ]
    threes = [
        remote(win.at[base + c], win.at[base + c], send3.at[c], recv3.at[c], {"grp": 1 - grp})
        for c in range(mine)
    ]
    reach = pl.ds(pl.multiple_of((1 - grp) * (width // 2 - 128), 128), width // 2 + 128)
    zeros = [
        remote(
            s_ref.at[part, pl.ds(HALF, HALF), reach],
            source.at[pl.ds(part * HALF, HALF), reach],
            send0.at[part], recv0.at[part], {"fft": 1 - fft},
        )
        for part in range(2)
    ]
    for copy in zeros:
        copy.start()

    def columns(value):
        high = value.astype(jnp.bfloat16)
        rounded = high.astype(jnp.float32)
        lane = lax.broadcasted_iota(jnp.int32, value.shape, 1)
        mixed = jnp.where(lane < GRID, rounded, value - rounded).astype(jnp.bfloat16)
        return jnp.concatenate([mixed, high], axis=1)

    y_cols[...] = columns(hat_ref[:, 0:128] * weight_ref[...])
    z_wave[...] = dot(columns(hat_ref[:, 128:256]), yt_ref[chunks])
    x_high, x_low = split(x_ref[...])
    atoms = x_ref.shape[1]
    for part in range(2):
        xt_high, xt_low = split(ft_ref[part * ROWS : (part + 1) * ROWS, 0:GRID])
        left = dot(xt_high, x_high) + dot(xt_low, x_high) + dot(xt_high, x_low)
        high, low = split(left)
        l_high[:, part * atoms : (part + 1) * atoms] = high
        l_low[:, part * atoms : (part + 1) * atoms] = low

    def fold(c):
        chunk = base + c
        window = pl.ds(pl.multiple_of((2 * (chunks - 1) - 2 * chunk) * 128, 128), 384)
        high, low = split(source[:, window])
        both = jnp.concatenate([high, low], axis=0)
        flipped = dot(both[:, 0:256], yt_ref[chunks + 1, :, 0:LANES])
        flipped += dot(both[:, 256:384], yt_ref[chunks + 1, 0:128, LANES : 2 * LANES])
        mirrored = dot(yt_ref[chunks + 1, 128:192, LANES : LANES + 128], flipped.astype(jnp.bfloat16))
        lanes = pl.ds(pl.multiple_of(chunk * LANES, LANES), LANES)
        own[c, 0:32] = s_ref[0, 0:32, lanes] + mirrored[0:32]
        own[c, 32:64] = s_ref[1, 0:32, lanes] + mirrored[32:64]
        row = lax.broadcasted_iota(jnp.int32, (8, LANES), 0)
        re, im = s_ref[0, 32:40, lanes][0:1], s_ref[1, 32:40, lanes][0:1]
        own[c, 64:72] = jnp.where(row == 0, re, jnp.where(row == 1, im, 0.0))

    def ligand(chunk):
        y_wave = dot(y_cols[...], yt_ref[chunk])
        y_re, y_im = y_wave[:, :LANES], y_wave[:, LANES:]
        z_re, z_im = z_wave[:, :LANES], z_wave[:, LANES:]
        re_high, re_low = split(y_re * z_re - y_im * z_im)
        im_high, im_low = split(y_re * z_im + y_im * z_re)
        v_high = jnp.concatenate([re_high, im_high], axis=0)
        v_low = jnp.concatenate([re_low, im_low], axis=0)
        lig[chunk] = (
            dot(l_high[...], v_high) + dot(l_low[...], v_high) + dot(l_high[...], v_low)
        )

    t_high, t_low = split(ft_ref[2 * ROWS : 2 * ROWS + 2 * GRID, 0:ROWS])

    def product(chunk):
        l_re, l_im = lig[chunk, 0:32], lig[chunk, 32:64]
        w_re, w_im = win[chunk, 0:32], win[chunk, 32:64]
        tail_l, tail_w = lig[chunk, 64:72], win[chunk, 64:72]
        a, b = tail_l[0:1], tail_l[1:2]
        c, d = tail_w[0:1], tail_w[1:2]
        row = lax.broadcasted_iota(jnp.int32, (8, LANES), 0)
        tail = jnp.where(row == 0, a * c - b * d, jnp.where(row == 1, a * d + b * c, 0.0))
        whole = jnp.concatenate([l_re * w_re - l_im * w_im, l_re * w_im + l_im * w_re, tail], axis=0)
        p_high, p_low = split(whole)
        lanes = pl.ds(pl.multiple_of(chunk * LANES, LANES), LANES)
        out_ref[:, lanes] = dot(t_high, p_high) + dot(t_low, p_high) + dot(t_high, p_low)

    ligand(0)
    for copy in zeros:
        copy.wait_recv()
    for c in range(mine):
        fold(c)
        ones[c].start()
    ligand(1)
    ligand(2)
    for c in range(mine):
        ones[c].wait_recv()
        pair[c] = own[c] + first[c]
        twos[c].start()
        ligand(3 + c)
    ligand(7)
    for c in range(mine):
        twos[c].wait_recv()
        win[base + c] = own[c] + second[c]
        threes[c].start()
        product(base + c)
    for c in range(mine):
        threes[c].wait_recv()
        product((1 - grp) * mine + c)
    for copy in zeros + ones + twos + threes:
        copy.wait_send()


def turned_product(receptor, table, x_hat, hats, weights, width):
    index = np.arange(GRID)
    chunks = width // LANES
    lane = np.arange(width)
    cosine, sine = host_waves(index, lane // GRID)
    y_table = np.stack(
        [
            tripled(
                np.concatenate(
                    [t[:, c * LANES : (c + 1) * LANES] for t in (cosine, sine)], axis=1
                )
            )
            for c in range(chunks)
        ]
    )
    z_table = tripled(np.concatenate(host_waves(index, lane[:LANES] % GRID), axis=1))
    cosine, sine = host_waves(index, np.arange(HALF + 1))
    real = np.concatenate([cosine[:, :HALF], -sine[:, :HALF], cosine[:, HALF:], -sine[:, HALF:]], 1)
    imag = np.concatenate([sine[:, :HALF], cosine[:, :HALF], sine[:, HALF:], cosine[:, HALF:]], 1)
    turn = np.concatenate([real, imag], axis=0) / float(GRID**3)
    turn = np.pad(turn, ((0, 0), (0, ROWS - turn.shape[1]))).astype(np.float32)

    flip = np.zeros((384, LANES), np.float32)
    for m in range(LANES // GRID):
        for kz in range(GRID):
            flip[(4 - m) * GRID + (-kz) % GRID, m * GRID + kz] = 1.0
    flip = flip.astype(jnp.bfloat16)
    rows = np.zeros((2 * HALF, 2 * HALF), np.float32)
    for kx in range(1, HALF):
        rows[kx, HALF - kx] = 1.0
        rows[HALF + kx, 2 * HALF - kx] = -1.0
    rows = np.concatenate([rows, rows], axis=1).astype(jnp.bfloat16)
    moves = np.zeros((1,) + y_table.shape[1:], jnp.bfloat16)
    moves[0, :, :LANES] = flip[:256]
    moves[0, :128, LANES:] = flip[256:]
    moves[0, 128:192, LANES : LANES + 128] = rows
    constants = np.concatenate([y_table, z_table[None], moves], axis=0)
    floats = np.zeros((2 * ROWS + 2 * GRID, 128), np.float32)
    floats[: 2 * ROWS, :GRID] = table.reshape(2 * ROWS, GRID)
    floats[2 * ROWS :, :ROWS] = turn
    atoms = hats.shape[0]
    piece = (ROWS, LANES)
    half = chunks // 2
    return pl.pallas_call(
        functools.partial(window_kernel, lax.axis_size("rec")),
        out_shape=jax.ShapeDtypeStruct((2 * GRID, width), jnp.float32),
        in_specs=[pl.BlockSpec(memory_space=pltpu.VMEM)] * 6,
        out_specs=pl.BlockSpec(memory_space=pltpu.VMEM),
        scratch_shapes=[
            pltpu.VMEM((2 * HALF, width + 128), jnp.float32),
            pltpu.VMEM((half,) + piece, jnp.float32),
            pltpu.VMEM((half,) + piece, jnp.float32),
            pltpu.VMEM((half,) + piece, jnp.float32),
            pltpu.VMEM((half,) + piece, jnp.float32),
            pltpu.VMEM((chunks,) + piece, jnp.float32),
            pltpu.VMEM((chunks,) + piece, jnp.float32),
            pltpu.VMEM((atoms, 4 * GRID), jnp.bfloat16),
            pltpu.VMEM((atoms, 2 * LANES), jnp.float32),
            pltpu.VMEM((ROWS, 2 * atoms), jnp.bfloat16),
            pltpu.VMEM((ROWS, 2 * atoms), jnp.bfloat16),
        ]
        + [pltpu.SemaphoreType.DMA((2,))] * 2
        + [pltpu.SemaphoreType.DMA((half,))] * 6,
        compiler_params=pltpu.CompilerParams(
            collective_id=0, has_side_effects=True, vmem_limit_bytes=40 * 1024 * 1024
        ),
    )(
        receptor, jnp.asarray(constants), jnp.asarray(floats), x_hat, hats, weights,
    )


def hats_of(record, rotations, ligand_coords, atom_types, channel_weights):
    table_rows = rotations.shape[0]
    picks = (record[:, None] == jnp.arange(table_rows, dtype=jnp.int32)[None, :]).astype(
        jnp.float32
    )
    matrix = jnp.dot(picks, rotations.reshape(table_rows, 9), precision=HIGHEST)[0]
    kinds = channel_weights.shape[0]
    type_hot = (atom_types[:, None] == jnp.arange(kinds, dtype=jnp.int32)[None, :]).astype(
        jnp.float32
    )
    odd = (jnp.arange(2 * GRID, dtype=jnp.int32) * lax.axis_index("fft")) % 2
    sign = 1.0 - 2.0 * odd.astype(jnp.float32)[None, :]
    weights = jnp.dot(
        type_hot, jnp.broadcast_to(channel_weights, (kinds, 2 * GRID)) * sign, precision=HIGHEST
    )
    coords = ligand_coords.astype(jnp.float32) * (1.0 / 256.0)
    matrix = matrix.reshape(3, 3)
    center = 0.5 * GRID
    cells = jnp.arange(GRID, dtype=jnp.float32)
    offset = center - jnp.concatenate([cells] * 4)
    spread = jnp.repeat(matrix[1:].T, 2 * GRID, axis=1)
    hats = jnp.maximum(
        0.0, 1.0 - jnp.abs(jnp.dot(coords.T, spread, precision=HIGHEST) + offset[None, :])
    )
    x_places = jnp.dot(jnp.broadcast_to(matrix[0], (GRID, 3)), coords, precision=HIGHEST)
    x_hat = jnp.maximum(0.0, 1.0 - jnp.abs(x_places + (center - cells)[:, None]))
    cosine, sine = host_waves(np.arange(HALF + 1), np.arange(GRID))
    none = np.zeros((6, GRID))
    meet_re = np.concatenate([cosine[:HALF], sine[:HALF], cosine[HALF:], sine[HALF:], none], 0)
    meet_im = np.concatenate([-sine[:HALF], cosine[:HALF], -sine[HALF:], cosine[HALF:], none], 0)
    table = np.stack([meet_re, meet_im])
    return table, x_hat, hats, weights


def body(record_ids, rotations, ligand_coords, atom_types, channel_weights, receptor_spectra):
    width = receptor_spectra.shape[-1]
    slab = GRID // lax.axis_size("fft")
    record = from_behind(record_ids, "rec", 2)
    parts = hats_of(record, rotations, ligand_coords, atom_types, channel_weights)
    turned = turned_product(receptor_spectra[0, 0], *parts, width).reshape(1, 2, GRID, width)
    index = np.arange(GRID)
    halves = lax.all_to_all(turned, "fft", split_axis=2, concat_axis=3, tiled=True)
    volume = halves.reshape(2, slab, GRID, GRID)
    cosine, sine = host_waves(index, index)
    z_turn = jnp.asarray(np.stack([cosine, -sine]), jnp.float32)
    y_all = np.stack([np.stack([cosine, -sine]), np.stack([sine, cosine])])

    def scores(y_turn):
        in_y = jnp.einsum("dcky,cxkz->dxyz", y_turn, volume, precision=HIGH)
        part = jnp.einsum("dxyz,dzt->xyt", in_y, z_turn, precision=HIGH)
        return part.reshape(1, slab, y_turn.shape[3] * GRID)

    count = lax.axis_size("chan")
    if count != 2:
        return lax.psum_scatter(scores(jnp.asarray(y_all, jnp.float32)), "chan", scatter_dimension=2, tiled=True)
    halves_y = jnp.asarray(np.stack([y_all[..., :HALF], y_all[..., HALF:]]), jnp.float32)
    me = lax.axis_index("chan")
    near = lax.dynamic_index_in_dim(halves_y, me, 0, keepdims=False)
    far = lax.dynamic_index_in_dim(halves_y, 1 - me, 0, keepdims=False)
    arrived = from_behind(scores(far), "chan", 1)
    return scores(near) + arrived


def solution(mesh):
    in_specs = (
        P(("grp", "rec")),
        P(),
        P(None, "grp"),
        P("grp"),
        P(None, "chan"),
        P("rec", "chan", None, None, "fft"),
    )
    out_specs = P(("grp", "rec"), "fft", "chan")
    return jax.shard_map(body, mesh=mesh, in_specs=in_specs, out_specs=out_specs, check_vma=False)
```
